32 devices in a mesh: groups: 2 (over y), tiles: 4 (over z), rhs: 2 (over x), sub: 2 (over core).
Axes of the slice: x: 2, y: 2, z: 4, core: 2. Of those that a mesh axis runs over, the one named last changes fastest.
Arguments:
- sources: bfloat16 [256, 8192], P('rhs', ('groups', 'tiles', 'sub')), parts along dimension 1, may hold values from -6 to 6
- basis_out: bfloat16 [384, 64, 512], P(('groups', 'tiles', 'rhs', 'sub')), parts along dimension 0, may hold values from -0.15625 to 0.15625
- basis_in: bfloat16 [384, 64, 512], P(('groups', 'tiles', 'rhs', 'sub')), parts along dimension 0, may hold values from -0.25 to 0.25
- tile_rank: int32 [384], P(('groups', 'tiles', 'rhs', 'sub')), parts along dimension 0, may hold values from 1 to 64, as said below
- tile_row: int32 [384], P(('groups', 'tiles', 'rhs', 'sub')), parts along dimension 0, may hold values from 0 to 7
- tile_col: int32 [384], P(('groups', 'tiles', 'rhs', 'sub')), parts along dimension 0, may hold values from 0 to 7
- near_blocks: bfloat16 [16, 16, 512, 512], P(('groups', 'tiles', 'sub')), parts along dimension 0, may hold values from -0.0625 to 0.0625
- near_col: int32 [16, 16], P(('groups', 'tiles', 'sub')), parts along dimension 0, may hold values from 0 to 7
- jacobi_inverse: bfloat16 [64, 128, 128], P(('groups', 'tiles', 'sub')), parts along dimension 0
Outputs:
- first_result: bfloat16 [256, 8192], P('rhs', ('groups', 'tiles', 'sub')), parts along dimension 1
- second_result: bfloat16 [256, 8192], P('rhs', ('groups', 'tiles', 'sub')), parts along dimension 1
The draws below stay inside these ranges and needn't reach their ends.
There are 2 independent parts, one for each index of `groups`. The reference program is written for one: setup_inputs(seed, part) draws one part's arguments, and reference() takes and returns one part's arrays. A program takes and returns all parts, laid end to end along the dimension named above; each array names one. Nothing has to cross between parts.
Inputs may be any that keep to these rules, and one draw needn't show every extreme that they name: `tile_rank`: every rank lies in 1 to 64, and some tile has rank 64.
All inputs are finite; a program needn't handle non-finite values.
Results may differ from the reference program's by a relative error of at most 0.03.
Values may be sent and summed in bfloat16 or wider, within the bound.
A program may use at most 128 MiB of HBM per device.

```python
import jax
import jax.numpy as jnp
from jax import lax

BLK = 512
RMAX = 64
JB = 128
NRHS = 256
NEAR = 16
NB_DEV = 1
TILE_DEV = 12
NB = 8
NPAN = 4096
NT = 192
NG = 32
N_RHS = 2


def draw_tile_rank(key, part):
    first_key = jax.random.fold_in(key, 11)
    second_key = jax.random.fold_in(key, 12)
    ranks = jax.random.randint(first_key, (NT,), 1, RMAX + 1, dtype=jnp.int32)
    position = jax.random.randint(second_key, (), 0, NT, dtype=jnp.int32)
    return jnp.where(jnp.arange(NT, dtype=jnp.int32) == position, RMAX, ranks).astype(jnp.int32)


def draw_jacobi_inverse(key, part):
    noise_key = jax.random.fold_in(key, 21)
    noise = jax.random.normal(noise_key, (NG, JB, JB), jnp.float32) * 0.5
    identity = jnp.eye(JB, dtype=jnp.float32)[None, :, :]
    return (identity + noise / JB ** 0.5).astype(jnp.bfloat16)


def plant(drawn, rng, smallest, top_value):
    place = [jax.random.randint(jax.random.fold_in(rng, axis), (), 0, length) for axis, length in enumerate(drawn.shape)]
    widest = drawn.shape.index(max(drawn.shape))
    next_to = place[:widest] + [(place[widest] + 1) % drawn.shape[widest]] + place[widest + 1:]
    return drawn.at[tuple(place)].set(smallest).at[tuple(next_to)].set(top_value)


def shard_levels(own_key, dims, shards, smallest, top_value):
    loudness = 1.0
    for dim, blocks in shards:
        draws = jax.random.uniform(jax.random.fold_in(jax.random.fold_in(own_key, 6), dim), (blocks,), jnp.float32, smallest / len(shards), top_value / len(shards))
        loudness = loudness * jnp.repeat(jnp.exp(draws), dims[dim] // blocks).reshape((-1,) + (1,) * (len(dims) - 1 - dim))
    return loudness


def centred(stream_key, dims, width, most, cuts=(), kind=jnp.bfloat16):
    drawn = width * jax.random.normal(stream_key, dims, jnp.float32)
    if cuts:
        drawn = drawn * shard_levels(stream_key, dims, cuts, -0.22, 0.18)
    return jnp.clip(drawn, -most, most).astype(kind)


def setup_inputs(seed: int = 0, part: int = 0) -> dict:
    keys = jax.random.split(jax.random.key(seed), 10)
    own_keys = jax.random.split(jax.random.fold_in(keys[9], part), 10)
    sources = centred(own_keys[0], (NRHS, NPAN), 1.0, 6.0, ((0, 2), (1, 8)))
    basis_out = centred(own_keys[1], (NT, RMAX, BLK), (RMAX * TILE_DEV * N_RHS // NB_DEV) ** -0.5, 0.15625, ((0, 16),))
    basis_in = centred(own_keys[2], (NT, RMAX, BLK), BLK ** -0.5, 0.25, ((0, 16),))
    tile_rank = draw_tile_rank(jax.random.fold_in(jax.random.fold_in(keys[9], part), 71), part)
    tile_row = plant(jax.random.randint(own_keys[4], (NT,), 0, NB), jax.random.fold_in(own_keys[4], 1), 0, NB - 1).astype(jnp.int32)
    tile_col = plant(jax.random.randint(own_keys[5], (NT,), 0, NB), jax.random.fold_in(own_keys[5], 1), 0, NB - 1).astype(jnp.int32)
    near_blocks = centred(own_keys[6], (NB, NEAR, BLK, BLK), (NEAR * BLK) ** -0.5, 0.0625, ((0, 8),))
    near_col = plant(jax.random.randint(own_keys[7], (NB, NEAR), 0, NB), jax.random.fold_in(own_keys[7], 1), 0, NB - 1).astype(jnp.int32)
    jacobi_inverse = draw_jacobi_inverse(jax.random.fold_in(jax.random.fold_in(keys[9], part), 71), part)
    return dict(sources=sources, basis_out=basis_out, basis_in=basis_in, tile_rank=tile_rank, tile_row=tile_row, tile_col=tile_col, near_blocks=near_blocks, near_col=near_col, jacobi_inverse=jacobi_inverse)


def apply_operator(vector, basis_out, basis_in, tile_rank, tile_row, tile_col, near_blocks, near_col):
    blocks = vector.reshape(NRHS, NB, BLK).transpose(1, 0, 2)

    def add_tile(running, index):
        coefficients = jnp.dot(blocks[tile_col[index]], basis_in[index].T, preferred_element_type=jnp.float32)
        kept_mask = jnp.arange(RMAX, dtype=jnp.int32) < tile_rank[index]
        coefficients = jnp.where(kept_mask[None, :], coefficients, jnp.zeros_like(coefficients)).astype(jnp.bfloat16)
        contrib = jnp.dot(coefficients, basis_out[index], preferred_element_type=jnp.float32)
        return running.at[tile_row[index]].add(contrib), None

    far_field, unused = lax.scan(add_tile, jnp.zeros((NB, NRHS, BLK), jnp.float32), jnp.arange(NT, dtype=jnp.int32))

    def near_row(index):
        picked = blocks[near_col[index]].astype(jnp.float32)
        return jnp.einsum('kcq,kpq->cp', picked, near_blocks[index].astype(jnp.float32))

    near_field = lax.map(near_row, jnp.arange(NB, dtype=jnp.int32))
    summed = (far_field + near_field).astype(jnp.bfloat16)
    return summed.transpose(1, 0, 2).reshape(NRHS, NPAN)


def precondition(field, jacobi_inverse):
    grouped = field.reshape(NRHS, NG, JB).astype(jnp.float32)
    result = jnp.einsum('cgq,gpq->cgp', grouped, jacobi_inverse.astype(jnp.float32))
    return result.astype(jnp.bfloat16).reshape(NRHS, NPAN)


def reference(sources, basis_out, basis_in, tile_rank, tile_row, tile_col, near_blocks, near_col, jacobi_inverse):
    first_result = precondition(apply_operator(sources, basis_out, basis_in, tile_rank, tile_row, tile_col, near_blocks, near_col), jacobi_inverse)
    second_result = precondition(apply_operator(first_result, basis_out, basis_in, tile_rank, tile_row, tile_col, near_blocks, near_col), jacobi_inverse)
    return (first_result, second_result)
```

```python
import functools

import jax
import jax.numpy as jnp
from jax import lax
from jax.experimental import pallas as pl
from jax.experimental.pallas import tpu as pltpu
from jax.sharding import PartitionSpec as P

MESH = pl.DeviceIdType.MESH
F32 = jnp.float32
BF16 = jnp.bfloat16
NT = (((1,), (1,)), ((), ()))


def dot_nt(a, b):
    return lax.dot_general(a, b, NT, preferred_element_type=F32)


def kernel(
    T,
    R,
    tile_col,
    near_col,
    src,
    basis_out,
    basis_in,
    onehot,
    near_hbm,
    jacobi,
    out0,
    out1,
    v0,
    v1,
    coef,
    fa,
    fd,
    fx,
    fz,
    nacc,
    near,
    near_sem,
    vz_send,
    vz_recv,
    vx_send,
    vx_recv,
    vd_send,
    vd_recv,
    fd_send,
    fd_recv,
    fx_send,
    fx_recv,
    fz_send,
    fz_recv,
):
    t = lax.axis_index("tiles")
    r = lax.axis_index("rhs")
    s = lax.axis_index("sub")
    M, B = src.shape
    n_tiles, rank, _ = basis_in.shape
    n_near = near_hbm.shape[0]
    has_left, has_right = t > 0, t < T - 1
    sibling = {"sub": 1 - s}
    partners = [lax.rem(r + k, R) for k in range(1, R)]

    def copy(src_ref, dst_ref, send, recv, device):
        return pltpu.make_async_remote_copy(
            src_ref=src_ref,
            dst_ref=dst_ref,
            send_sem=send,
            recv_sem=recv,
            device_id=device,
            device_id_type=MESH,
        )

    near_copy = pltpu.make_async_copy(near_hbm, near, near_sem)
    near_copy.start()

    barrier = pltpu.get_barrier_semaphore()

    @pl.when(has_left)
    def _():
        pl.semaphore_signal(barrier, inc=1, device_id={"tiles": t - 1}, device_id_type=MESH)

    @pl.when(has_right)
    def _():
        pl.semaphore_signal(barrier, inc=1, device_id={"tiles": t + 1}, device_id_type=MESH)

    for q in partners:
        pl.semaphore_signal(barrier, inc=1, device_id={"rhs": q}, device_id_type=MESH)
    pl.semaphore_signal(barrier, inc=1, device_id=sibling, device_id_type=MESH)

    neighbours = (t + T - 1) // T + (2 * T - 2 - t) // T
    pl.semaphore_wait(barrier, R + neighbours)

    def gather(v):
        def z_copy(tt, side):
            ref = v.at[tt * 2 + s, r]
            return copy(ref, ref, vz_send.at[side, tt], vz_recv.at[tt], {"tiles": t + 2 * side - 1})

        def x_copy(tt, q):
            ref = v.at[tt * 2 + s, r]
            return copy(ref, ref, vx_send.at[tt, q], vx_recv.at[tt, r], {"rhs": q})

        def x_arrival(tt, q):
            ref = v.at[tt * 2 + s, q]
            return copy(ref, ref, vx_send.at[tt, q], vx_recv.at[tt, q], {"rhs": q})

        def d_copy(tt, q):
            ref = v.at[tt * 2 + s, q]
            return copy(ref, ref, vd_send.at[tt, q], vd_recv.at[tt, q], sibling)

        def d_arrival(tt, q):
            ref = v.at[tt * 2 + 1 - s, q]
            return copy(ref, ref, vd_send.at[tt, q], vd_recv.at[tt, q], sibling)

        def spread(tt):
            for q in partners:
                x_copy(tt, q).start()
            d_copy(tt, r).start()

        def pass_on(tt):
            for q in partners:
                x_arrival(tt, q).wait_recv()
                d_copy(tt, q).start()

        @pl.when(has_left)
        def _():
            z_copy(t, 0).start()

        @pl.when(has_right)
        def _():
            z_copy(t, 1).start()

        spread(t)
        for d in range(1, T + 1):
            if d < T:

                @pl.when(t - d >= 0)
                def _():
                    z_copy(t - d, 1).wait_recv()

                    @pl.when(has_right)
                    def _():
                        z_copy(t - d, 1).start()

                    spread(t - d)

                @pl.when(t + d < T)
                def _():
                    z_copy(t + d, 0).wait_recv()

                    @pl.when(has_left)
                    def _():
                        z_copy(t + d, 0).start()

                    spread(t + d)

            if d == 1:
                pass_on(t)
            else:

                @pl.when(t - (d - 1) >= 0)
                def _():
                    pass_on(t - (d - 1))

                @pl.when(t + (d - 1) < T)
                def _():
                    pass_on(t + (d - 1))

        for tt in range(T):
            for q in range(R):
                d_arrival(tt, q).wait_recv()

        def finish():
            for tt in range(T):

                @pl.when(has_left & (tt >= t))
                def _():
                    z_copy(tt, 0).wait_send()

                @pl.when(has_right & (tt <= t))
                def _():
                    z_copy(tt, 1).wait_send()

                for q in partners:
                    x_copy(tt, q).wait_send()
                for q in range(R):
                    d_copy(tt, q).wait_send()

        return finish

    def fd_copy(tt):
        return copy(fa.at[tt * 2 + 1 - s], fd.at[tt], fd_send.at[tt], fd_recv.at[tt], sibling)

    def fx_copy(tt, q):
        return copy(
            fa.at[tt * 2 + s, q], fx.at[r, tt], fx_send.at[tt, q], fx_recv.at[tt, r], {"rhs": q}
        )

    def fx_arrival(tt, q):
        return copy(
            fa.at[tt * 2 + s, q], fx.at[q, tt], fx_send.at[tt, q], fx_recv.at[tt, q], {"rhs": q}
        )

    def fz_copy(tt, side):
        return copy(
            fa.at[tt * 2 + s, r],
            fz.at[side, tt],
            fz_send.at[tt],
            fz_recv.at[side, tt],
            {"tiles": t + 2 * side - 1},
        )

    sign = 2 * ((2 * t) // T) - 1

    def nth(p):
        return (t + sign * (1 + p) + 2 * T) % T

    def far_block(i):
        masked = coef[...] * onehot[i].astype(BF16)
        block = jnp.dot(masked, basis_out[...], preferred_element_type=F32)
        fa[i] = block.astype(BF16).reshape(R, M, B)

    def far_start(v):
        lane = lax.broadcasted_iota(jnp.int32, (R * M, 2 * rank), 1)
        for k in range(0, n_tiles, 2):
            pair = basis_in[k : k + 2].reshape(2 * rank, B)
            c0 = dot_nt(v[tile_col[k]].reshape(R * M, B), pair)
            c1 = dot_nt(v[tile_col[k + 1]].reshape(R * M, B), pair)
            coef[:, k * rank : (k + 2) * rank] = jnp.where(lane < rank, c0, c1).astype(BF16)

        @pl.loop(0, T)
        def _(p):
            tt = nth(p)
            far_block(tt * 2 + 1 - s)
            fd_copy(tt).start()

        @pl.loop(0, T)
        def _(p):
            tt = nth(p)
            far_block(tt * 2 + s)
            fd_copy(tt).wait_recv()
            fa[tt * 2 + s] = (fa[tt * 2 + s].astype(F32) + fd[tt].astype(F32)).astype(BF16)
            for q in partners:
                fx_copy(tt, q).start()

    def near_field(v):
        total = None
        for k in range(n_near):
            term = dot_nt(v[near_col[k], r], near[k])
            if k == 0:
                nacc[...] = term
            else:
                nacc[...] += term

    def far_end():
        def summed(tt):
            acc = fa[tt * 2 + s, r].astype(F32)
            for q in partners:
                fx_arrival(tt, q).wait_recv()
                acc += fx[q, tt].astype(F32)
            fa[tt * 2 + s, r] = acc.astype(BF16)

        def absorb(tt, side):
            fz_copy(tt, side).wait_recv()
            acc = fa[tt * 2 + s, r].astype(F32) + fz[side, tt].astype(F32)
            fa[tt * 2 + s, r] = acc.astype(BF16)

        for d in range(T - 1, 0, -1):

            @pl.when(t + d < T)
            def _():
                summed(t + d)

                @pl.when(has_left)
                def _():
                    absorb(t + d, 1)

                fz_copy(t + d, 1).start()

            @pl.when(t - d >= 0)
            def _():
                summed(t - d)

                @pl.when(has_right)
                def _():
                    absorb(t - d, 0)

                fz_copy(t - d, 0).start()

        acc = nacc[...] + fa[t * 2 + s, r].astype(F32)
        for q in partners:
            fx_arrival(t, q).wait_recv()
            acc += fx[q, t].astype(F32)
        nacc[...] = acc

        @pl.when(has_left)
        def _():
            fz_copy(t, 1).wait_recv()
            nacc[...] += fz[1, t].astype(F32)

        @pl.when(has_right)
        def _():
            fz_copy(t, 0).wait_recv()
            nacc[...] += fz[0, t].astype(F32)

    def far_finish():
        for tt in range(T):
            fd_copy(tt).wait_send()
            for q in partners:
                fx_copy(tt, q).wait_send()

            @pl.when(tt > t)
            def _():
                fz_copy(tt, 1).wait_send()

            @pl.when(tt < t)
            def _():
                fz_copy(tt, 0).wait_send()

    def precondition(out):
        for g in range(jacobi.shape[0]):
            jb = jacobi.shape[1]
            field = nacc[:, g * jb : (g + 1) * jb].astype(BF16)
            out[:, g * jb : (g + 1) * jb] = dot_nt(field, jacobi[g]).astype(BF16)

    for app, (v, out) in enumerate(((v0, out0), (v1, out1))):
        v[t * 2 + s, r] = (src if app == 0 else out0)[...]
        finish = gather(v)
        if app == 1:
            far_finish()
        far_start(v)
        if app == 0:
            near_copy.wait()
        near_field(v)
        finish()
        far_end()
        precondition(out)
    far_finish()


def local(
    T,
    R,
    sources,
    basis_out,
    basis_in,
    tile_rank,
    tile_row,
    tile_col,
    near_blocks,
    near_col,
    jacobi_inverse,
):
    n_tiles, rank, B = basis_in.shape
    M = sources.shape[0]
    NB = 2 * T
    n_near = near_blocks.shape[1]
    kept = jnp.arange(rank, dtype=jnp.int32)[None, :] < tile_rank[:, None]
    row = jnp.where(kept, tile_row[:, None], -1).reshape(1, 1, n_tiles * rank)
    onehot = (row == jnp.arange(NB, dtype=jnp.int32)[:, None, None]).astype(F32)
    vmem = pl.BlockSpec(memory_space=pltpu.VMEM)
    smem = pl.BlockSpec(memory_space=pltpu.SMEM)
    dma = pltpu.SemaphoreType.DMA
    out = jax.ShapeDtypeStruct((M, B), BF16)
    return pl.pallas_call(
        functools.partial(kernel, T, R),
        out_shape=(out, out),
        in_specs=[smem, smem, vmem, vmem, vmem, vmem, pl.BlockSpec(memory_space=pl.ANY), vmem],
        out_specs=(vmem, vmem),
        scratch_shapes=[
            pltpu.VMEM((NB, R, M, B), BF16),
            pltpu.VMEM((NB, R, M, B), BF16),
            pltpu.VMEM((R * M, n_tiles * rank), BF16),
            pltpu.VMEM((NB, R, M, B), BF16),
            pltpu.VMEM((T, R, M, B), BF16),
            pltpu.VMEM((R, T, M, B), BF16),
            pltpu.VMEM((2, T, M, B), BF16),
            pltpu.VMEM((M, B), F32),
            pltpu.VMEM((n_near, B, B), BF16),
            dma,
            dma((2, T)),
            dma((T,)),
            dma((T, R)),
            dma((T, R)),
            dma((T, R)),
            dma((T, R)),
            dma((T,)),
            dma((T,)),
            dma((T, R)),
            dma((T, R)),
            dma((T,)),
            dma((2, T)),
        ],
        compiler_params=pltpu.CompilerParams(
            collective_id=0, has_side_effects=True, vmem_limit_bytes=60 * 1024 * 1024
        ),
        name="operator_twice",
    )(
        tile_col,
        near_col.reshape(n_near),
        sources,
        basis_out.reshape(n_tiles * rank, B),
        basis_in,
        onehot,
        near_blocks.reshape(n_near, B, B),
        jacobi_inverse,
    )


def solution(mesh):
    return jax.shard_map(
        functools.partial(local, mesh.shape["tiles"], mesh.shape["rhs"]),
        mesh=mesh,
        in_specs=(
            P("rhs", ("groups", "tiles", "sub")),
            P(("groups", "tiles", "rhs", "sub"), None, None),
            P(("groups", "tiles", "rhs", "sub"), None, None),
            P(("groups", "tiles", "rhs", "sub")),
            P(("groups", "tiles", "rhs", "sub")),
            P(("groups", "tiles", "rhs", "sub")),
            P(("groups", "tiles", "sub"), None, None, None),
            P(("groups", "tiles", "sub"), None),
            P(("groups", "tiles", "sub"), None, None),
        ),
        out_specs=(P("rhs", ("groups", "tiles", "sub")), P("rhs", ("groups", "tiles", "sub"))),
        check_vma=False,
    )
```

```python
import functools

import jax
import jax.numpy as jnp
from jax import lax
from jax.experimental import pallas as pl
from jax.experimental.pallas import tpu as pltpu
from jax.sharding import PartitionSpec as P

MESH = pl.DeviceIdType.MESH
F32 = jnp.float32
BF16 = jnp.bfloat16
NT = (((1,), (1,)), ((), ()))


def dot_nt(a, b):
    return lax.dot_general(a, b, NT, preferred_element_type=F32)


def kernel(
    T,
    R,
    C,
    tile_rank,
    tile_row,
    tile_col,
    near_col,
    src,
    basis_out,
    basis_in,
    near_hbm,
    jacobi,
    out0,
    out1,
    v0,
    v1,
    coef,
    rows,
    fa,
    fd,
    fx,
    fz,
    nacc,
    near,
    near_sem,
    vz_send,
    vz_recv,
    vx_send,
    vx_recv,
    vd_send,
    vd_recv,
    fd_send,
    fd_recv,
    fx_send,
    fx_recv,
    fz_send,
    fz_recv,
):
    t = lax.axis_index("tiles")
    r = lax.axis_index("rhs")
    s = lax.axis_index("sub")
    M, B = src.shape
    n_tiles, rank, _ = basis_in.shape
    n_near = near_hbm.shape[0]
    has_left, has_right = t > 0, t < T - 1
    sibling = {"sub": 1 - s}
    partners = [lax.rem(r + k, R) for k in range(1, R)]

    def copy(src_ref, dst_ref, send, recv, device):
        return pltpu.make_async_remote_copy(
            src_ref=src_ref,
            dst_ref=dst_ref,
            send_sem=send,
            recv_sem=recv,
            device_id=device,
            device_id_type=MESH,
        )

    near_copy = pltpu.make_async_copy(near_hbm, near, near_sem)

    barrier = pltpu.get_barrier_semaphore()

    @pl.when(has_left)
    def _():
        pl.semaphore_signal(barrier, inc=1, device_id={"tiles": t - 1}, device_id_type=MESH)

    @pl.when(has_right)
    def _():
        pl.semaphore_signal(barrier, inc=1, device_id={"tiles": t + 1}, device_id_type=MESH)

    for q in partners:
        pl.semaphore_signal(barrier, inc=1, device_id={"rhs": q}, device_id_type=MESH)
    pl.semaphore_signal(barrier, inc=1, device_id=sibling, device_id_type=MESH)

    near_copy.start()
    lane = lax.broadcasted_iota(jnp.int32, (1, 2 * rank), 1)
    first = lane < rank
    for k in range(0, n_tiles, 2):
        row = jnp.where(first, tile_row[k], tile_row[k + 1])
        top = jnp.where(first, tile_rank[k], tile_rank[k + 1] + rank)
        rows[:, k * rank : (k + 2) * rank] = jnp.where(lane < top, row, -1)

    neighbours = (t + T - 1) // T + (2 * T - 2 - t) // T
    pl.semaphore_wait(barrier, R + neighbours)

    m = M // C

    def part(c):
        return pl.ds(c * m, m)

    class Gather:
        def __init__(self, v):
            self.v = v

        def z(self, tt, side, c):
            ref = self.v.at[tt * 2 + s, r, part(c)]
            return copy(
                ref, ref, vz_send.at[side, tt, c], vz_recv.at[tt, c], {"tiles": t + 2 * side - 1}
            )

        def x(self, tt, q, c):
            ref = self.v.at[tt * 2 + s, r, part(c)]
            return copy(ref, ref, vx_send.at[tt, q, c], vx_recv.at[tt, r, c], {"rhs": q})

        def x_arrival(self, tt, q, c):
            ref = self.v.at[tt * 2 + s, q, part(c)]
            return copy(ref, ref, vx_send.at[tt, q, c], vx_recv.at[tt, q, c], {"rhs": q})

        def d(self, tt, q, core):
            ref = self.v.at[tt * 2 + core, q]
            return copy(ref, ref, vd_send.at[tt, q], vd_recv.at[tt, q], sibling)

        def pass_on(self, tt):
            for q in partners:
                for c in range(C):
                    self.x_arrival(tt, q, c).wait_recv()
                self.d(tt, q, s).start()

        def begin(self):
            for c in range(C):

                @pl.when(has_left)
                def _():
                    self.z(t, 0, c).start()

                @pl.when(has_right)
                def _():
                    self.z(t, 1, c).start()

                for q in partners:
                    self.x(t, q, c).start()
            self.d(t, r, s).start()

        def forward(self, tt, side, c, onward):
            self.z(tt, side, c).wait_recv()

            @pl.when(onward)
            def _():
                self.z(tt, side, c).start()

            for q in partners:
                self.x(tt, q, c).start()
            if c == C - 1:
                self.d(tt, r, s).start()

        def run(self):
            for d in range(1, T + 1):
                for c in range(C if d < T else 0):

                    @pl.when(t - d >= 0)
                    def _():
                        self.forward(t - d, 1, c, has_right)

                    @pl.when(t + d < T)
                    def _():
                        self.forward(t + d, 0, c, has_left)

                if d == 1:
                    self.pass_on(t)
                else:

                    @pl.when(t - (d - 1) >= 0)
                    def _():
                        self.pass_on(t - (d - 1))

                    @pl.when(t + (d - 1) < T)
                    def _():
                        self.pass_on(t + (d - 1))

            for tt in range(T):
                for q in range(R):
                    self.d(tt, q, 1 - s).wait_recv()

        def finish(self):
            for tt in range(T):
                for c in range(C):

                    @pl.when(has_left & (tt >= t))
                    def _():
                        self.z(tt, 0, c).wait_send()

                    @pl.when(has_right & (tt <= t))
                    def _():
                        self.z(tt, 1, c).wait_send()

                    for q in partners:
                        self.x(tt, q, c).wait_send()
                for q in range(R):
                    self.d(tt, q, s).wait_send()

    def fd_copy(tt):
        return copy(fa.at[tt * 2 + 1 - s], fd.at[tt], fd_send.at[tt], fd_recv.at[tt], sibling)

    def fx_copy(tt, q, c):
        return copy(
            fa.at[tt * 2 + s, q, part(c)],
            fx.at[r, tt, part(c)],
            fx_send.at[tt, q, c],
            fx_recv.at[tt, r, c],
            {"rhs": q},
        )

    def fx_arrival(tt, q, c):
        return copy(
            fa.at[tt * 2 + s, q, part(c)],
            fx.at[q, tt, part(c)],
            fx_send.at[tt, q, c],
            fx_recv.at[tt, q, c],
            {"rhs": q},
        )

    def fz_copy(tt, side, c):
        return copy(
            fa.at[tt * 2 + s, r, part(c)],
            fz.at[side, tt, part(c)],
            fz_send.at[tt, c],
            fz_recv.at[side, tt, c],
            {"tiles": t + 2 * side - 1},
        )

    sign = 2 * ((2 * t) // T) - 1

    def nth(p):
        return (t + sign * (1 + p) + 2 * T) % T

    def far_block(i):
        masked = coef[...] * (rows[...] == i).astype(F32).astype(BF16)
        block = jnp.dot(masked, basis_out[...], preferred_element_type=F32)
        fa[i] = block.astype(BF16).reshape(R, M, B)

    def far_start(v):
        for k in range(0, n_tiles, 2):
            pair = basis_in[k : k + 2].reshape(2 * rank, B)
            picked = [v[tile_col[k + j]].reshape(R * M, B) for j in range(2)]
            both = dot_nt(jnp.concatenate(picked, axis=0), pair)
            coef[:, k * rank : (k + 2) * rank] = jnp.where(
                first, both[: R * M], both[R * M :]
            ).astype(BF16)

        @pl.loop(0, T)
        def _(p):
            tt = nth(p)
            far_block(tt * 2 + 1 - s)
            fd_copy(tt).start()

        @pl.loop(0, T)
        def _(p):
            tt = nth(p)
            far_block(tt * 2 + s)
            fd_copy(tt).wait_recv()
            fa[tt * 2 + s] = (fa[tt * 2 + s].astype(F32) + fd[tt].astype(F32)).astype(BF16)
            for q in partners:
                for c in range(C):
                    fx_copy(tt, q, c).start()

    def near_field(v):
        total = None
        for k in range(n_near):
            term = dot_nt(v[near_col[k], r], near[k])
            if k == 0:
                nacc[...] = term
            else:
                nacc[...] += term

    def far_end():
        def settle(tt, side, c, more):
            here = part(c)
            acc = fa[tt * 2 + s, r, here].astype(F32)
            for q in partners:
                fx_arrival(tt, q, c).wait_recv()
                acc += fx[q, tt, here].astype(F32)
            fa[tt * 2 + s, r, here] = acc.astype(BF16)

            @pl.when(more)
            def _():
                fz_copy(tt, side, c).wait_recv()
                total = fa[tt * 2 + s, r, here].astype(F32) + fz[side, tt, here].astype(F32)
                fa[tt * 2 + s, r, here] = total.astype(BF16)

            fz_copy(tt, side, c).start()

        for d in range(T - 1, 0, -1):
            for c in range(C):

                @pl.when(t + d < T)
                def _():
                    settle(t + d, 1, c, has_left)

                @pl.when(t - d >= 0)
                def _():
                    settle(t - d, 0, c, has_right)

        for c in range(C):
            here = part(c)
            acc = nacc[here] + fa[t * 2 + s, r, here].astype(F32)
            for q in partners:
                fx_arrival(t, q, c).wait_recv()
                acc += fx[q, t, here].astype(F32)
            nacc[here] = acc

        for c in range(C):
            here = part(c)

            @pl.when(has_left)
            def _():
                fz_copy(t, 1, c).wait_recv()
                nacc[here] += fz[1, t, here].astype(F32)

            @pl.when(has_right)
            def _():
                fz_copy(t, 0, c).wait_recv()
                nacc[here] += fz[0, t, here].astype(F32)

    def far_finish():
        for tt in range(T):
            fd_copy(tt).wait_send()
            for c in range(C):
                for q in partners:
                    fx_copy(tt, q, c).wait_send()

                @pl.when(tt > t)
                def _():
                    fz_copy(tt, 1, c).wait_send()

                @pl.when(tt < t)
                def _():
                    fz_copy(tt, 0, c).wait_send()

    one, two = Gather(v0), Gather(v1)
    v0[t * 2 + s, r] = src[...]
    one.begin()
    one.run()
    far_start(v0)
    near_copy.wait()
    near_field(v0)
    far_end()
    result = precondition(nacc[...].astype(BF16), jacobi)
    v1[t * 2 + s, r] = result
    one.finish()
    two.begin()
    out0[...] = result
    two.run()
    far_finish()
    far_start(v1)
    near_field(v1)
    far_end()
    out1[...] = nacc[...].astype(BF16)
    two.finish()
    far_finish()


def precondition(field, jacobi):
    jb = jacobi.shape[1]
    groups = [
        dot_nt(field[:, g * jb : (g + 1) * jb], jacobi[g]).astype(BF16)
        for g in range(jacobi.shape[0])
    ]
    return jnp.concatenate(groups, axis=1)


def last_kernel(first, field, jacobi, out0, out1):
    out0[...] = first[...]
    out1[...] = precondition(field[...], jacobi)


def local(
    T,
    R,
    sources,
    basis_out,
    basis_in,
    tile_rank,
    tile_row,
    tile_col,
    near_blocks,
    near_col,
    jacobi_inverse,
):
    n_tiles, rank, B = basis_in.shape
    M = sources.shape[0]
    NB = 2 * T
    C = 2
    n_near = near_blocks.shape[1]
    vmem = pl.BlockSpec(memory_space=pltpu.VMEM)
    smem = pl.BlockSpec(memory_space=pltpu.SMEM)
    dma = pltpu.SemaphoreType.DMA
    out = jax.ShapeDtypeStruct((M, B), BF16)
    first, field = pl.pallas_call(
        functools.partial(kernel, T, R, C),
        out_shape=(out, out),
        in_specs=[smem] * 4 + [vmem] * 3 + [pl.BlockSpec(memory_space=pl.ANY), vmem],
        out_specs=(vmem, vmem),
        scratch_shapes=[
            pltpu.VMEM((NB, R, M, B), BF16),
            pltpu.VMEM((NB, R, M, B), BF16),
            pltpu.VMEM((R * M, n_tiles * rank), BF16),
            pltpu.VMEM((1, n_tiles * rank), jnp.int32),
            pltpu.VMEM((NB, R, M, B), BF16),
            pltpu.VMEM((T, R, M, B), BF16),
            pltpu.VMEM((R, T, M, B), BF16),
            pltpu.VMEM((2, T, M, B), BF16),
            pltpu.VMEM((M, B), F32),
            pltpu.VMEM((n_near, B, B), BF16),
            dma,
            dma((2, T, C)),
            dma((T, C)),
            dma((T, R, C)),
            dma((T, R, C)),
            dma((T, R)),
            dma((T, R)),
            dma((T,)),
            dma((T,)),
            dma((T, R, C)),
            dma((T, R, C)),
            dma((T, C)),
            dma((2, T, C)),
        ],
        compiler_params=pltpu.CompilerParams(
            collective_id=0, has_side_effects=True, vmem_limit_bytes=60 * 1024 * 1024
        ),
        name="operator_twice",
    )(
        tile_rank,
        tile_row,
        tile_col,
        near_col.reshape(n_near),
        sources,
        basis_out.reshape(n_tiles * rank, B),
        basis_in,
        near_blocks.reshape(n_near, B, B),
        jacobi_inverse,
    )
    return pl.pallas_call(
        last_kernel,
        out_shape=(out, out),
        in_specs=[vmem] * 3,
        out_specs=(vmem, vmem),
        name="last_precondition",
    )(first, field, jacobi_inverse)


def solution(mesh):
    return jax.shard_map(
        functools.partial(local, mesh.shape["tiles"], mesh.shape["rhs"]),
        mesh=mesh,
        in_specs=(
            P("rhs", ("groups", "tiles", "sub")),
            P(("groups", "tiles", "rhs", "sub"), None, None),
            P(("groups", "tiles", "rhs", "sub"), None, None),
            P(("groups", "tiles", "rhs", "sub")),
            P(("groups", "tiles", "rhs", "sub")),
            P(("groups", "tiles", "rhs", "sub")),
            P(("groups", "tiles", "sub"), None, None, None),
            P(("groups", "tiles", "sub"), None),
            P(("groups", "tiles", "sub"), None, None),
        ),
        out_specs=(P("rhs", ("groups", "tiles", "sub")), P("rhs", ("groups", "tiles", "sub"))),
        check_vma=False,
    )
```

```python
import functools

import jax
import jax.numpy as jnp
from jax import lax
from jax.experimental import pallas as pl
from jax.experimental.pallas import tpu as pltpu
from jax.sharding import PartitionSpec as P

MESH = pl.DeviceIdType.MESH
F32 = jnp.float32
BF16 = jnp.bfloat16
NT = (((1,), (1,)), ((), ()))


def dot_nt(a, b):
    return lax.dot_general(a, b, NT, preferred_element_type=F32)


def kernel(
    T,
    R,
    C,
    tile_rank,
    tile_row,
    tile_col,
    near_col,
    src,
    basis_out,
    basis_in,
    near_hbm,
    jacobi,
    out0,
    out1,
    v0,
    v1,
    coef,
    rows,
    fa,
    fd,
    fx,
    fz,
    nacc,
    near,
    near_sem,
    vz_send,
    vz_recv,
    vx_send,
    vx_recv,
    vd_send,
    vd_recv,
    fd_send,
    fd_recv,
    fx_send,
    fx_recv,
    fz_send,
    fz_recv,
):
    t = lax.axis_index("tiles")
    r = lax.axis_index("rhs")
    s = lax.axis_index("sub")
    M, B = src.shape
    n_tiles, rank, _ = basis_in.shape
    n_near = near_hbm.shape[0]
    has_left, has_right = t > 0, t < T - 1
    sibling = {"sub": 1 - s}
    partners = [lax.rem(r + k, R) for k in range(1, R)]

    def copy(src_ref, dst_ref, send, recv, device):
        return pltpu.make_async_remote_copy(
            src_ref=src_ref,
            dst_ref=dst_ref,
            send_sem=send,
            recv_sem=recv,
            device_id=device,
            device_id_type=MESH,
        )

    near_copy = pltpu.make_async_copy(near_hbm, near, near_sem)

    barrier = pltpu.get_barrier_semaphore()

    @pl.when(has_left)
    def _():
        pl.semaphore_signal(barrier, inc=1, device_id={"tiles": t - 1}, device_id_type=MESH)

    @pl.when(has_right)
    def _():
        pl.semaphore_signal(barrier, inc=1, device_id={"tiles": t + 1}, device_id_type=MESH)

    for q in partners:
        pl.semaphore_signal(barrier, inc=1, device_id={"rhs": q}, device_id_type=MESH)
    pl.semaphore_signal(barrier, inc=1, device_id=sibling, device_id_type=MESH)

    near_copy.start()
    lane = lax.broadcasted_iota(jnp.int32, (1, 2 * rank), 1)
    first = lane < rank
    for k in range(0, n_tiles, 2):
        row = jnp.where(first, tile_row[k], tile_row[k + 1])
        top = jnp.where(first, tile_rank[k], tile_rank[k + 1] + rank)
        rows[:, k * rank : (k + 2) * rank] = jnp.where(lane < top, row, -1)

    neighbours = (t + T - 1) // T + (2 * T - 2 - t) // T
    pl.semaphore_wait(barrier, R + neighbours)

    m = M // C

    def part(c):
        return pl.ds(c * m, m)

    class Gather:
        def __init__(self, v):
            self.v = v

        def z(self, tt, side, c):
            ref = self.v.at[tt * 2 + s, r, part(c)]
            return copy(
                ref, ref, vz_send.at[side, tt, c], vz_recv.at[tt, c], {"tiles": t + 2 * side - 1}
            )

        def x(self, tt, q, c):
            ref = self.v.at[tt * 2 + s, r, part(c)]
            return copy(ref, ref, vx_send.at[tt, q, c], vx_recv.at[tt, r, c], {"rhs": q})

        def x_arrival(self, tt, q, c):
            ref = self.v.at[tt * 2 + s, q, part(c)]
            return copy(ref, ref, vx_send.at[tt, q, c], vx_recv.at[tt, q, c], {"rhs": q})

        def d(self, tt, q, core):
            ref = self.v.at[tt * 2 + core, q]
            return copy(ref, ref, vd_send.at[tt, q], vd_recv.at[tt, q], sibling)

        def pass_on(self, tt):
            for q in partners:
                for c in range(C):
                    self.x_arrival(tt, q, c).wait_recv()
                self.d(tt, q, s).start()

        def begin(self):
            for c in range(C):

                @pl.when(has_left)
                def _():
                    self.z(t, 0, c).start()

                @pl.when(has_right)
                def _():
                    self.z(t, 1, c).start()

                for q in partners:
                    self.x(t, q, c).start()
            self.d(t, r, s).start()

        def forward(self, tt, side, c, onward):
            self.z(tt, side, c).wait_recv()

            @pl.when(onward)
            def _():
                self.z(tt, side, c).start()

            for q in partners:
                self.x(tt, q, c).start()
            if c == C - 1:
                self.d(tt, r, s).start()

        def run(self):
            for d in range(1, T + 1):
                for c in range(C if d < T else 0):

                    @pl.when(t - d >= 0)
                    def _():
                        self.forward(t - d, 1, c, has_right)

                    @pl.when(t + d < T)
                    def _():
                        self.forward(t + d, 0, c, has_left)

                if d == 1:
                    self.pass_on(t)
                else:

                    @pl.when(t - (d - 1) >= 0)
                    def _():
                        self.pass_on(t - (d - 1))

                    @pl.when(t + (d - 1) < T)
                    def _():
                        self.pass_on(t + (d - 1))

            for tt in range(T):
                for q in range(R):
                    self.d(tt, q, 1 - s).wait_recv()

        def finish(self):
            for tt in range(T):
                for c in range(C):

                    @pl.when(has_left & (tt >= t))
                    def _():
                        self.z(tt, 0, c).wait_send()

                    @pl.when(has_right & (tt <= t))
                    def _():
                        self.z(tt, 1, c).wait_send()

                    for q in partners:
                        self.x(tt, q, c).wait_send()
                for q in range(R):
                    self.d(tt, q, s).wait_send()

    def fd_copy(tt):
        return copy(fa.at[tt * 2 + 1 - s], fd.at[tt], fd_send.at[tt], fd_recv.at[tt], sibling)

    def fx_copy(tt, q, c):
        return copy(
            fa.at[tt * 2 + s, q, part(c)],
            fx.at[r, tt, part(c)],
            fx_send.at[tt, q, c],
            fx_recv.at[tt, r, c],
            {"rhs": q},
        )

    def fx_arrival(tt, q, c):
        return copy(
            fa.at[tt * 2 + s, q, part(c)],
            fx.at[q, tt, part(c)],
            fx_send.at[tt, q, c],
            fx_recv.at[tt, q, c],
            {"rhs": q},
        )

    def fz_copy(tt, side, c):
        return copy(
            fa.at[tt * 2 + s, r, part(c)],
            fz.at[side, tt, part(c)],
            fz_send.at[tt, c],
            fz_recv.at[side, tt, c],
            {"tiles": t + 2 * side - 1},
        )

    sign = 2 * ((2 * t) // T) - 1

    def nth(p):
        return (t + sign * (1 + p) + 2 * T) % T

    def far_block(i):
        masked = coef[...] * (rows[...] == i).astype(F32).astype(BF16)
        block = jnp.dot(masked, basis_out[...], preferred_element_type=F32)
        fa[i] = block.astype(BF16).reshape(R, M, B)

    def far_start(v):
        for k in range(0, n_tiles, 2):
            pair = basis_in[k : k + 2].reshape(2 * rank, B)
            picked = [v[tile_col[k + j]].reshape(R * M, B) for j in range(2)]
            both = dot_nt(jnp.concatenate(picked, axis=0), pair)
            coef[:, k * rank : (k + 2) * rank] = jnp.where(
                first, both[: R * M], both[R * M :]
            ).astype(BF16)

        @pl.loop(0, T)
        def _(p):
            tt = nth(p)
            far_block(tt * 2 + 1 - s)
            fd_copy(tt).start()

        @pl.loop(0, T)
        def _(p):
            tt = nth(p)
            far_block(tt * 2 + s)
            fd_copy(tt).wait_recv()
            fa[tt * 2 + s] = (fa[tt * 2 + s].astype(F32) + fd[tt].astype(F32)).astype(BF16)
            for q in partners:
                for c in range(C):
                    fx_copy(tt, q, c).start()

    def near_field(v):
        total = None
        for k in range(n_near):
            term = dot_nt(v[near_col[k], r], near[k])
            if k == 0:
                nacc[...] = term
            else:
                nacc[...] += term

    def far_end():
        def settle(tt, side, c, more):
            here = part(c)
            acc = fa[tt * 2 + s, r, here].astype(F32)
            for q in partners:
                fx_arrival(tt, q, c).wait_recv()
                acc += fx[q, tt, here].astype(F32)
            fa[tt * 2 + s, r, here] = acc.astype(BF16)

            @pl.when(more)
            def _():
                fz_copy(tt, side, c).wait_recv()
                total = fa[tt * 2 + s, r, here].astype(F32) + fz[side, tt, here].astype(F32)
                fa[tt * 2 + s, r, here] = total.astype(BF16)

            fz_copy(tt, side, c).start()

        for d in range(T - 1, 0, -1):
            for c in range(C):

                @pl.when(t + d < T)
                def _():
                    settle(t + d, 1, c, has_left)

                @pl.when(t - d >= 0)
                def _():
                    settle(t - d, 0, c, has_right)

        for c in range(C):
            here = part(c)
            acc = nacc[here] + fa[t * 2 + s, r, here].astype(F32)
            for q in partners:
                fx_arrival(t, q, c).wait_recv()
                acc += fx[q, t, here].astype(F32)
            nacc[here] = acc

        for c in range(C):
            here = part(c)

            @pl.when(has_left)
            def _():
                fz_copy(t, 1, c).wait_recv()
                nacc[here] += fz[1, t, here].astype(F32)

            @pl.when(has_right)
            def _():
                fz_copy(t, 0, c).wait_recv()
                nacc[here] += fz[0, t, here].astype(F32)

    def far_finish():
        for tt in range(T):
            fd_copy(tt).wait_send()
            for c in range(C):
                for q in partners:
                    fx_copy(tt, q, c).wait_send()

                @pl.when(tt > t)
                def _():
                    fz_copy(tt, 1, c).wait_send()

                @pl.when(tt < t)
                def _():
                    fz_copy(tt, 0, c).wait_send()

    one, two = Gather(v0), Gather(v1)
    v0[t * 2 + s, r] = src[...]
    one.begin()
    one.run()
    far_start(v0)
    near_copy.wait()
    near_field(v0)
    far_end()
    result = precondition(nacc[...].astype(BF16), jacobi)
    v1[t * 2 + s, r] = result
    one.finish()
    two.begin()
    out0[...] = result
    two.run()
    far_finish()
    far_start(v1)
    near_field(v1)
    far_end()
    out1[...] = nacc[...].astype(BF16)
    two.finish()
    far_finish()


def precondition(field, jacobi):
    jb = jacobi.shape[1]
    groups = [
        dot_nt(field[:, g * jb : (g + 1) * jb], jacobi[g]).astype(BF16)
        for g in range(jacobi.shape[0])
    ]
    return jnp.concatenate(groups, axis=1)


def last_kernel(first, field, jacobi, out0, out1):
    out0[...] = first[...]
    out1[...] = precondition(field[...], jacobi)


def local(
    T,
    R,
    sources,
    basis_out,
    basis_in,
    tile_rank,
    tile_row,
    tile_col,
    near_blocks,
    near_col,
    jacobi_inverse,
):
    n_tiles, rank, B = basis_in.shape
    M = sources.shape[0]
    NB = 2 * T
    C = max(1, M // 32)
    n_near = near_blocks.shape[1]
    vmem = pl.BlockSpec(memory_space=pltpu.VMEM)
    smem = pl.BlockSpec(memory_space=pltpu.SMEM)
    dma = pltpu.SemaphoreType.DMA
    out = jax.ShapeDtypeStruct((M, B), BF16)
    first, field = pl.pallas_call(
        functools.partial(kernel, T, R, C),
        out_shape=(out, out),
        in_specs=[smem] * 4 + [vmem] * 3 + [pl.BlockSpec(memory_space=pl.ANY), vmem],
        out_specs=(vmem, vmem),
        scratch_shapes=[
            pltpu.VMEM((NB, R, M, B), BF16),
            pltpu.VMEM((NB, R, M, B), BF16),
            pltpu.VMEM((R * M, n_tiles * rank), BF16),
            pltpu.VMEM((1, n_tiles * rank), jnp.int32),
            pltpu.VMEM((NB, R, M, B), BF16),
            pltpu.VMEM((T, R, M, B), BF16),
            pltpu.VMEM((R, T, M, B), BF16),
            pltpu.VMEM((2, T, M, B), BF16),
            pltpu.VMEM((M, B), F32),
            pltpu.VMEM((n_near, B, B), BF16),
            dma,
            dma((2, T, C)),
            dma((T, C)),
            dma((T, R, C)),
            dma((T, R, C)),
            dma((T, R)),
            dma((T, R)),
            dma((T,)),
            dma((T,)),
            dma((T, R, C)),
            dma((T, R, C)),
            dma((T, C)),
            dma((2, T, C)),
        ],
        compiler_params=pltpu.CompilerParams(
            collective_id=0, has_side_effects=True, vmem_limit_bytes=60 * 1024 * 1024
        ),
        name="operator_twice",
    )(
        tile_rank,
        tile_row,
        tile_col,
        near_col.reshape(n_near),
        sources,
        basis_out.reshape(n_tiles * rank, B),
        basis_in,
        near_blocks.reshape(n_near, B, B),
        jacobi_inverse,
    )
    return pl.pallas_call(
        last_kernel,
        out_shape=(out, out),
        in_specs=[vmem] * 3,
        out_specs=(vmem, vmem),
        name="last_precondition",
    )(first, field, jacobi_inverse)


def solution(mesh):
    return jax.shard_map(
        functools.partial(local, mesh.shape["tiles"], mesh.shape["rhs"]),
        mesh=mesh,
        in_specs=(
            P("rhs", ("groups", "tiles", "sub")),
            P(("groups", "tiles", "rhs", "sub"), None, None),
            P(("groups", "tiles", "rhs", "sub"), None, None),
            P(("groups", "tiles", "rhs", "sub")),
            P(("groups", "tiles", "rhs", "sub")),
            P(("groups", "tiles", "rhs", "sub")),
            P(("groups", "tiles", "sub"), None, None, None),
            P(("groups", "tiles", "sub"), None),
            P(("groups", "tiles", "sub"), None, None),
        ),
        out_specs=(P("rhs", ("groups", "tiles", "sub")), P("rhs", ("groups", "tiles", "sub"))),
        check_vma=False,
    )
```
